128 devices in a mesh: ctr: 8 (over x_hi, y), row: 4 (over z), col: 4 (over x_lo, core).
Axes of the slice: x: 4 (x_hi: 2, x_lo: 2; x = x_hi * 2 + x_lo), y: 4, z: 4, core: 2. Of those that a mesh axis runs over, the one named last changes fastest.
Arguments:
- amps: bfloat16 [4, 1024, 16, 1024], P('row', 'ctr', 'col'), may hold values from -6 to 6
- w_cycle: bfloat16 [16, 1024, 4, 1024], P('ctr', 'row', 'col'), may hold values from -0.125 to 0.125
- w_cross: bfloat16 [16, 1024, 4, 1024], P('ctr', 'row', 'col'), may hold values from -0.125 to 0.125
- occ_sizes: int32 [8], replicated, may hold values from 1 to 50, 200 in all
- virt_sizes: int32 [8], replicated, may hold values from 1 to 256, 1024 in all
- slab_occ: int32 [4], replicated, may hold values from 0 to 199
- k_occ: int32 [16], replicated, may hold values from 0 to 199
- j_occ: int32 [4], replicated, may hold values from 0 to 199
Outputs:
- update: bfloat16 [4, 1024, 4, 1024], P('row', 'ctr', 'col')
The draws below stay inside these ranges and needn't reach their ends.
Inputs may be any that keep to these rules, and one draw needn't show every extreme that they name: occ_sizes sum to 200. virt_sizes sum to 1024.
All inputs are finite; a program needn't handle non-finite values.
Results may differ from the reference program's by a relative error of at most 0.001.
Values may be sent and summed in bfloat16 or wider, within the bound.
No kernel may reach another device: no remote copies, remote signals or barrier semaphores. Data moves between devices by JAX's collectives and lax.ppermute only.
A program may use at most 64 MiB of HBM per device.

```python
import math
import jax
import jax.numpy as jnp
import numpy as np

O = 200
V = 1024
NI = 4
NK = 16
NJ = 4


def place_ends(result, key, least, high):
    index_at = [jax.random.randint(jax.random.fold_in(key, axis), (), 0, length) for axis, length in enumerate(result.shape)]
    widest = result.shape.index(max(result.shape))
    next_to = index_at[:widest] + [(index_at[widest] + 1) % result.shape[widest]] + index_at[widest + 1:]
    return result.at[tuple(index_at)].set(least).at[tuple(next_to)].set(high)


def steps_of(own_key, shape, pieces, smallest, top_value):
    level, own = 1.0, jax.random.fold_in(own_key, 6)
    for axis_at, blocks in pieces:
        steps = jnp.exp(jax.random.uniform(jax.random.fold_in(own, axis_at), (blocks,), jnp.float32, smallest / len(pieces), top_value / len(pieces)))
        level = level * jnp.repeat(steps, shape[axis_at] // blocks).reshape([-1 if axis == axis_at else 1 for axis in range(len(shape))])
    return level


def profile(amount, total, bound, skew):
    loads = [(1 << 20) // math.isqrt(rank ** skew) + 1 for rank in range(2, amount + 1)]
    spare, given = total - bound - (amount - 1), [1] * (amount - 1)
    while spare > 0:
        free = [i for i in range(amount - 1) if given[i] < bound]
        whole, budget = sum([loads[i] for i in free]), spare
        for i in free:
            addition = min(bound - given[i], max(1, budget * loads[i] // whole), spare)
            given[i] = given[i] + addition
            spare = spare - addition
    return np.array([bound] + given)


def ragged(stream_key, number_of, total, limit, slope):
    if number_of == 2:
        one = jax.random.randint(stream_key, (), max(1, total - limit), min(limit, total - 1) + 1)
        return jnp.stack([one, total - one])
    lengths = jnp.asarray(profile(number_of, total, limit, slope), jnp.int32)
    couples = (number_of - 1) // 2
    source_of, taker = lengths[1:1 + 2 * couples:2], lengths[2:2 + 2 * couples:2]
    margin = jnp.minimum(source_of - 1, limit - taker)
    passed = jax.random.randint(jax.random.fold_in(stream_key, 1), (couples,), 0, 1 << 20) % (margin + 1)
    lengths = lengths.at[1:1 + 2 * couples:2].set(source_of - passed).at[2:2 + 2 * couples:2].set(taker + passed)
    return lengths[jax.random.permutation(jax.random.fold_in(stream_key, 2), number_of)]


def centred(key, extent, scale, bound, shards=(), held_as=jnp.bfloat16):
    values = jax.random.normal(key, extent, jnp.float32) * scale
    if len(shards) > 0:
        values = steps_of(key, extent, shards, -0.22, 0.18) * values
    return jnp.clip(values, min=-bound, max=bound).astype(held_as)


def setup_inputs(seed: int = 0) -> dict:
    seeds = jax.random.split(jax.random.key(seed), 9)
    amps = centred(seeds[0], (NI, V, NK, V), 1.0, 6.0, ((0, 4), (1, 8), (2, 4)))
    w_cycle = centred(seeds[1], (NK, V, NJ, V), (NK * V // 8) ** -0.5, 0.125, ((0, 8), (1, 4), (2, 4)))
    w_cross = centred(seeds[2], (NK, V, NJ, V), (NK * V // 8) ** -0.5, 0.125, ((0, 8), (1, 4), (2, 4)))
    occ_sizes = ragged(seeds[3], 8, O, O // 4, 1).astype(jnp.int32)
    virt_sizes = ragged(seeds[4], 8, V, V // 4, 1).astype(jnp.int32)
    slab_occ = place_ends(jax.random.randint(seeds[5], (NI,), 0, O), jax.random.fold_in(seeds[5], 1), 0, O - 1).astype(jnp.int32)
    k_occ = place_ends(jax.random.randint(seeds[6], (NK,), 0, O), jax.random.fold_in(seeds[6], 1), 0, O - 1).astype(jnp.int32)
    j_occ = place_ends(jax.random.randint(seeds[7], (NJ,), 0, O), jax.random.fold_in(seeds[7], 1), 0, O - 1).astype(jnp.int32)
    return {"amps": amps, "w_cycle": w_cycle, "w_cross": w_cross, "occ_sizes": occ_sizes, "virt_sizes": virt_sizes, "slab_occ": slab_occ, "k_occ": k_occ, "j_occ": j_occ}


def irreps_of(index, sizes):
    bounds = jnp.cumsum(sizes)[:7]
    return jnp.sum((index[..., None] >= bounds).astype(jnp.int32), axis=-1).astype(jnp.int32)


def reference(amps, w_cycle, w_cross, occ_sizes, virt_sizes, slab_occ, k_occ, j_occ):
    irr_i = irreps_of(slab_occ, occ_sizes)
    irr_k = irreps_of(k_occ, occ_sizes)
    irr_j = irreps_of(j_occ, occ_sizes)
    irr_v = irreps_of(jnp.arange(V, dtype=jnp.int32), virt_sizes)
    keep = jnp.bitwise_xor(jnp.bitwise_xor(irr_i[:, None, None, None], irr_v[None, :, None, None]), jnp.bitwise_xor(irr_k[None, None, :, None], irr_v[None, None, None, :])) == 0
    t_sym = jnp.where(keep, amps, jnp.zeros((), amps.dtype))
    left = t_sym.astype(jnp.float32).reshape(NI * V, NK * V)
    cycle = jnp.dot(left, w_cycle.astype(jnp.float32).reshape(NK * V, NJ * V), preferred_element_type=jnp.float32)
    swapped = jnp.transpose(t_sym, (0, 3, 2, 1)).astype(jnp.float32).reshape(NI * V, NK * V)
    crossed = jnp.dot(swapped, w_cross.astype(jnp.float32).reshape(NK * V, NJ * V), preferred_element_type=jnp.float32)
    total = (cycle + crossed).reshape(NI, V, NJ, V)
    out_keep = jnp.bitwise_xor(jnp.bitwise_xor(irr_i[:, None, None, None], irr_v[None, :, None, None]), jnp.bitwise_xor(irr_j[None, None, :, None], irr_v[None, None, None, :])) == 0
    return jnp.where(out_keep, total, jnp.zeros((), total.dtype)).astype(jnp.bfloat16)
```

```python
import jax
import jax.numpy as jnp
from jax import lax
from jax.sharding import PartitionSpec as P

FOLD = 256


def irreps_of(index, sizes):
    bounds = jnp.cumsum(sizes)[:7]
    return jnp.sum((index[..., None] >= bounds).astype(jnp.int32), axis=-1)


def fold(values, keep):
    kept = jnp.where(keep, values, jnp.zeros((), values.dtype))
    chunks = [kept[..., at : at + FOLD] for at in range(0, kept.shape[-1], FOLD)]
    return sum(chunks[1:], chunks[0])


def unfold(folded, keep):
    wide = jnp.concatenate([folded] * (keep.shape[-1] // FOLD), axis=-1)
    return jnp.where(keep, wide, jnp.zeros((), folded.dtype))


def shift(value, axis, count, step):
    return lax.ppermute(value, axis, [(at, (at + step) % count) for at in range(count)])


def swap(value, axis, count, mask):
    return lax.ppermute(value, axis, [(at, at ^ mask) for at in range(count)])


def on_device(amps, w_cycle, w_cross, occ_sizes, virt_sizes, slab_occ, k_occ, j_occ):
    ctr, row, col = lax.axis_index("ctr"), lax.axis_index("row"), lax.axis_index("col")
    virt = amps.shape[3]
    irr_v = irreps_of(jnp.arange(virt, dtype=jnp.int32), virt_sizes)
    irr_occ = irreps_of(jnp.concatenate([slab_occ, k_occ, j_occ]), occ_sizes)
    irr_i = lax.dynamic_slice_in_dim(irr_occ, row, 1)[0]
    irr_j = lax.dynamic_slice_in_dim(irr_occ, 20 + col, 1)[0]
    irr_kt = lax.dynamic_slice_in_dim(irr_occ, 4 + 4 * col, 4)
    irr_kw = lax.dynamic_slice_in_dim(irr_occ, 4 + 2 * ctr, 2)
    irr_a = lax.dynamic_slice_in_dim(irr_v, ctr * 128, 128)
    irr_c = lax.dynamic_slice_in_dim(irr_v, row * 256, 256)

    keep_w = (irr_kw ^ irr_j)[:, None, None] == (irr_c[:, None] ^ irr_v[None, :])[None]
    w = fold(w_cycle[:, :, 0, :], keep_w)
    u = fold(w_cross[:, :, 0, :], keep_w)
    w_up, u_down = shift(w, "row", 4, 1), shift(u, "row", 4, -1)
    w_down, u_up = shift(w, "row", 4, -1), shift(u, "row", 4, 1)
    w_far, u_far = shift(w_up, "row", 4, 1), shift(u_down, "row", 4, -1)

    keep_t = (irr_kt ^ irr_i)[:, None, None] == (irr_a[:, None] ^ irr_v[None, :])[None]
    t = fold(jnp.transpose(amps[0], (1, 0, 2)), keep_t)
    odd = ctr % 2
    arrived = []
    for flip in range(2):
        pairs = [
            (x * 4 + q, (2 * q + (x % 2 ^ flip)) * 4 + x // 2) for x in range(8) for q in range(4)
        ]
        piece = lax.dynamic_slice_in_dim(t, 2 * (odd ^ flip), 2)
        arrived.append(lax.ppermute(piece, ("ctr", "col"), pairs))
    quarter = jnp.stack(
        [
            jnp.where(odd == 0, arrived[0], arrived[1]),
            jnp.where(odd == 0, arrived[1], arrived[0]),
        ]
    )
    other = swap(quarter, "col", 4, 2)
    half = jnp.where(col // 2 == 0, jnp.stack([quarter, other]), jnp.stack([other, quarter]))
    there = swap(half, "col", 4, 1)
    odd_core = col % 2 == 1
    full = jnp.where(
        odd_core, jnp.stack([there, half], axis=1), jnp.stack([half, there], axis=1)
    )
    t_all = jnp.transpose(full.reshape(8, 2, 128, FOLD), (1, 0, 2, 3)).reshape(2, virt, FOLD)
    keep = (irr_kw ^ irr_i)[:, None, None] == (irr_v[:, None] ^ irr_v[None, :])[None]
    t_sym = unfold(t_all, keep)

    def laid(own, up, down, far):
        blocks = jnp.stack([own, up, far, down])
        order = (row - jnp.arange(4, dtype=jnp.int32)) % 4
        return jnp.transpose(blocks[order], (1, 0, 2, 3)).reshape(2, virt, FOLD)

    part = jnp.einsum(
        "kac,kcb->ab", t_sym, laid(w, w_up, w_down, w_far), preferred_element_type=jnp.float32
    ) + jnp.einsum(
        "kda,kdb->ab", t_sym, laid(u, u_up, u_down, u_far), preferred_element_type=jnp.float32
    )
    part = part.reshape(8, 128, FOLD)
    total = lax.dynamic_index_in_dim(part, ctr, 0, False)
    for mask in (4, 6, 5, 7, 2, 1, 3):
        total = total + swap(lax.dynamic_index_in_dim(part, ctr ^ mask, 0, False), "ctr", 8, mask)
    out_keep = (irr_a[:, None] ^ irr_v[None, :]) == (irr_i ^ irr_j)
    return unfold(total, out_keep).astype(jnp.bfloat16)[None, :, None, :]


def solution(mesh):
    return jax.shard_map(
        on_device,
        mesh=mesh,
        in_specs=(
            P("row", "ctr", "col", None),
            P("ctr", "row", "col", None),
            P("ctr", "row", "col", None),
            P(),
            P(),
            P(),
            P(),
            P(),
        ),
        out_specs=P("row", "ctr", "col", None),
        check_vma=False,
    )
```

```python
import functools

import jax
import jax.numpy as jnp
from jax import lax
from jax.experimental import pallas as pl
from jax.experimental.pallas import tpu as pltpu
from jax.sharding import PartitionSpec as P

FOLD = 256
SMEM = pl.BlockSpec(memory_space=pltpu.SMEM)
VMEM = pl.BlockSpec(memory_space=pltpu.VMEM)


def bounds_of(sizes_ref):
    total, bounds = sizes_ref[0], []
    for g in range(1, 8):
        bounds.append(total)
        total = total + sizes_ref[g]
    return bounds


def irrep(index, bounds):
    total = (index >= bounds[0]).astype(jnp.int32)
    for bound in bounds[1:]:
        total = total + (index >= bound).astype(jnp.int32)
    return total


def irrep_lanes(start, count, bounds):
    return irrep(lax.broadcasted_iota(jnp.int32, (1, count), 1) + start, bounds)


def irrep_rows(start, count, bounds):
    return irrep(lax.broadcasted_iota(jnp.int32, (count, 1), 0) + start, bounds)


def fold_of(load, want, lanes):
    total = None
    for at, irr in enumerate(lanes):
        kept = jnp.where(want == irr, load(at).astype(jnp.float32), 0.0)
        total = kept if total is None else total + kept
    return total


def fold_integrals(w_ref, u_ref, occ_ref, virt_ref, k_ref, j_ref, out_ref):
    ctr, row, col = lax.axis_index("ctr"), lax.axis_index("row"), lax.axis_index("col")
    occ, virt = bounds_of(occ_ref), bounds_of(virt_ref)
    lanes = [irrep_lanes(at * FOLD, FOLD, virt) for at in range(4)]
    rows = irrep_rows(row * 256, 256, virt)
    irr_j = irrep(j_ref[col], occ)
    for k in range(2):
        want = rows ^ (irr_j ^ irrep(k_ref[2 * ctr + k], occ))
        for n, ref in enumerate((w_ref, u_ref)):
            folded = fold_of(lambda at: ref[k, :, at * FOLD : (at + 1) * FOLD], want, lanes)
            out_ref[n, k] = folded.T.astype(out_ref.dtype)


def fold_amplitudes(t_ref, occ_ref, virt_ref, slab_ref, k_ref, out_ref):
    ctr, row, col = lax.axis_index("ctr"), lax.axis_index("row"), lax.axis_index("col")
    occ, virt = bounds_of(occ_ref), bounds_of(virt_ref)
    lanes = [irrep_lanes(at * FOLD, FOLD, virt) for at in range(4)]
    rows = irrep_rows(ctr * 128, 128, virt)
    irr_i = irrep(slab_ref[row], occ)
    for k in range(4):
        want = rows ^ (irr_i ^ irrep(k_ref[4 * col + k], occ))
        folded = fold_of(lambda at: t_ref[:, k, at * FOLD : (at + 1) * FOLD], want, lanes)
        out_ref[(ctr % 2) ^ (k // 2), k % 2] = folded.astype(out_ref.dtype)


def products(targets, *refs):
    (t0, t1, t2, t3, t4, own_ref, up_ref, down_ref, wfar_ref, ufar_ref, occ_ref, virt_ref, slab_ref, k_ref, out_ref, t_all) = refs
    ctr, row, col = lax.axis_index("ctr"), lax.axis_index("row"), lax.axis_index("col")
    occ, virt = bounds_of(occ_ref), bounds_of(virt_ref)
    odd, y = ctr % 2, ctr % 4
    for u in range(2):
        for k in range(2):
            t_all[k, 2 * col + (odd ^ u)] = (t0 if u == 0 else t1)[k]
            for flip, ref in ((2, t2), (1, t3), (3, t4)):
                t_all[k, 2 * (col ^ flip) + (odd ^ u)] = ref[u, k]
    irr_i = irrep(slab_ref[row], occ)
    away = [irr_i ^ irrep(k_ref[2 * ctr + k], occ) for k in range(2)]
    quarters = [row, (row + 3) % 4, (row + 1) % 4, (row + 2) % 4]
    w = [lambda k: own_ref[0, k], lambda k: up_ref[0, k], lambda k: down_ref[0, k], lambda k: wfar_ref[k]]
    u = [lambda k: own_ref[1, k], lambda k: up_ref[1, k], lambda k: down_ref[1, k], lambda k: ufar_ref[k]]
    q_lanes = [irrep_lanes(q * 256, 256, virt) for q in quarters]
    q_rows = [irrep_rows(q * 256, 256, virt) for q in quarters]
    dtype = t_all.dtype
    for at, ahead in enumerate(targets):
        to = (y + ahead) % 4
        a_rows = [irrep_rows((4 * h + to) * 128, 128, virt) for h in range(2)]
        a_lanes = [irrep_lanes((4 * h + to) * 128, 128, virt) for h in range(2)]
        total = jnp.zeros((FOLD, 256), jnp.float32)
        for k in range(2):
            left = [t_all[k, 4 * h + to].astype(jnp.float32) for h in range(2)]
            for n, q in enumerate(quarters):
                right = jnp.concatenate(
                    [jnp.where((a_rows[h] ^ away[k]) == q_lanes[n], left[h], 0.0) for h in range(2)], axis=0
                ).astype(dtype)
                total = total + lax.dot_general(
                    w[n](k), right, (((1,), (1,)), ((), ())), preferred_element_type=jnp.float32
                )
                both = t_all[k, pl.ds(2 * q, 2)].reshape(256, FOLD).astype(jnp.float32)
                half = jnp.where(to % 2 == 0, both[:, :128], both[:, 128:])
                right = jnp.concatenate(
                    [jnp.where((q_rows[n] ^ away[k]) == a_lanes[h], half, 0.0) for h in range(2)], axis=1
                ).astype(dtype)
                total = total + lax.dot_general(
                    u[n](k), right, (((1,), (0,)), ((), ())), preferred_element_type=jnp.float32
                )
        out_ref[at, 0] = total[:, :128]
        out_ref[at, 1] = total[:, 128:]


def finish(own_ref, up_ref, down_ref, across_ref, occ_ref, virt_ref, slab_ref, j_ref, out_ref):
    ctr, row, col = lax.axis_index("ctr"), lax.axis_index("row"), lax.axis_index("col")
    occ, virt = bounds_of(occ_ref), bounds_of(virt_ref)
    h = ctr // 4
    total = (own_ref[h] + up_ref[h] + down_ref[h] + across_ref[...]).T
    want = irrep_rows(ctr * 128, 128, virt) ^ (irrep(slab_ref[row], occ) ^ irrep(j_ref[col], occ))
    for at in range(4):
        kept = jnp.where(want == irrep_lanes(at * FOLD, FOLD, virt), total, 0.0)
        out_ref[:, at * FOLD : (at + 1) * FOLD] = kept.astype(out_ref.dtype)


def call(kernel, shape, dtype, arrays, scalars, scratch=(), flops=0, name=None):
    return pl.pallas_call(
        kernel,
        out_shape=jax.ShapeDtypeStruct(shape, dtype),
        in_specs=[VMEM] * len(arrays) + [SMEM] * len(scalars),
        out_specs=VMEM,
        scratch_shapes=scratch,
        compiler_params=pltpu.CompilerParams(vmem_limit_bytes=40 << 20),
        cost_estimate=pl.CostEstimate(flops=flops, bytes_accessed=1 << 20, transcendentals=0),
        name=name,
    )(*arrays, *scalars)


def shift(value, axis, count, step):
    return lax.ppermute(value, axis, [(at, (at + step) % count) for at in range(count)])


def shift_y(value, step):
    return lax.ppermute(value, "ctr", [(at, at // 4 * 4 + (at + step) % 4) for at in range(8)])


def swap(value, axis, count, mask):
    return lax.ppermute(value, axis, [(at, at ^ mask) for at in range(count)])


def on_device(amps, w_cycle, w_cross, occ_sizes, virt_sizes, slab_occ, k_occ, j_occ):
    bf16, f32 = jnp.bfloat16, jnp.float32
    own = call(
        fold_integrals, (2, 2, FOLD, 256), bf16, [w_cycle[:, :, 0], w_cross[:, :, 0]],
        [occ_sizes, virt_sizes, k_occ, j_occ], name="fold_integrals",
    )
    up, down = shift(own, "row", 4, 1), shift(own, "row", 4, -1)
    w_far, u_far = shift(up[0], "row", 4, 1), shift(down[1], "row", 4, -1)

    t = call(
        fold_amplitudes, (2, 2, 128, FOLD), bf16, [amps[0]],
        [occ_sizes, virt_sizes, slab_occ, k_occ], name="fold_amplitudes",
    )
    arrived = []
    for flip in range(2):
        pairs = [
            (x * 4 + q, (2 * q + (x % 2 ^ flip)) * 4 + x // 2) for x in range(8) for q in range(4)
        ]
        arrived.append(lax.ppermute(t[flip], ("ctr", "col"), pairs))
    quarter = jnp.stack(arrived)
    beside = swap(quarter, "col", 4, 2)
    there, beyond = swap(quarter, "col", 4, 1), swap(beside, "col", 4, 1)

    args = [*arrived, beside, there, beyond, own, up, down, w_far, u_far]
    scalars = [occ_sizes, virt_sizes, slab_occ, k_occ]

    def form(targets):
        return call(
            functools.partial(products, targets), (len(targets), 2, FOLD, 128), f32, args, scalars,
            [pltpu.VMEM((2, 8, 128, FOLD), bf16)], flops=len(targets) << 29, name="products",
        )

    far = form((2,))[0]
    near = form((1, 3, 0))
    from_below, from_above = shift_y(far[0], 1), shift_y(far[1], -1)
    low = shift_y(near[0].at[0].add(from_below), 1)
    high = shift_y(near[1].at[1].add(from_above), -1)
    other = 1 - lax.axis_index("ctr") // 4
    pick = lambda value: lax.dynamic_index_in_dim(value, other, 0, False)
    across = swap(pick(near[2]) + pick(low) + pick(high), "ctr", 8, 4)
    out = call(
        finish, (128, 4 * FOLD), bf16, [near[2], low, high, across],
        [occ_sizes, virt_sizes, slab_occ, j_occ], name="finish",
    )
    return out[None, :, None, :]


def solution(mesh):
    return jax.shard_map(
        on_device,
        mesh=mesh,
        in_specs=(
            P("row", "ctr", "col", None),
            P("ctr", "row", "col", None),
            P("ctr", "row", "col", None),
            P(),
            P(),
            P(),
            P(),
            P(),
        ),
        out_specs=P("row", "ctr", "col", None),
        check_vma=False,
    )
```

```python
import functools

import jax
import jax.numpy as jnp
from jax import lax
from jax.experimental import pallas as pl
from jax.experimental.pallas import tpu as pltpu
from jax.sharding import PartitionSpec as P

FOLD = 256
SMEM = pl.BlockSpec(memory_space=pltpu.SMEM)
VMEM = pl.BlockSpec(memory_space=pltpu.VMEM)


def bounds_of(sizes_ref):
    total, bounds = sizes_ref[0], []
    for g in range(1, 8):
        bounds.append(total)
        total = total + sizes_ref[g]
    return bounds


def irrep(index, bounds):
    total = (index >= bounds[0]).astype(jnp.int32)
    for bound in bounds[1:]:
        total = total + (index >= bound).astype(jnp.int32)
    return total


def irrep_lanes(start, count, bounds):
    return irrep(lax.broadcasted_iota(jnp.int32, (1, count), 1) + start, bounds)


def irrep_rows(start, count, bounds):
    return irrep(lax.broadcasted_iota(jnp.int32, (count, 1), 0) + start, bounds)


def fold_of(load, want, lanes):
    total = None
    for at, irr in enumerate(lanes):
        kept = jnp.where(want == irr, load(at).astype(jnp.float32), 0.0)
        total = kept if total is None else total + kept
    return total


def fold_integrals(w_hbm, u_hbm, *refs):
    small, (out_ref, w_ref, u_ref, *held, sems, small_sems) = refs[:4], refs[4:]
    fetch = [pltpu.make_async_copy(*pair, small_sems.at[n]) for n, pair in enumerate(zip(small, held))]
    copies = [
        [
            pltpu.make_async_copy(hbm.at[k], ref.at[k], sems.at[k, n])
            for n, (hbm, ref) in enumerate(((w_hbm, w_ref), (u_hbm, u_ref)))
        ]
        for k in range(2)
    ]
    for copy in [*fetch, *copies[0], *copies[1]]:
        copy.start()
    for copy in fetch:
        copy.wait()
    occ_ref, virt_ref, k_ref, j_ref = held
    ctr, row, col = lax.axis_index("ctr"), lax.axis_index("row"), lax.axis_index("col")
    occ, virt = bounds_of(occ_ref), bounds_of(virt_ref)
    lanes = [irrep_lanes(at * FOLD, FOLD, virt) for at in range(4)]
    rows = irrep_rows(row * 256, 256, virt)
    irr_j = irrep(j_ref[col], occ)
    for k in range(2):
        want = rows ^ (irr_j ^ irrep(k_ref[2 * ctr + k], occ))
        for n, ref in enumerate((w_ref, u_ref)):
            copies[k][n].wait()
            folded = fold_of(lambda at: ref[k, :, at * FOLD : (at + 1) * FOLD], want, lanes)
            out_ref[n, k] = folded.T.astype(out_ref.dtype)


def fold_amplitudes(t_ref, occ_ref, virt_ref, slab_ref, k_ref, out_ref):
    ctr, row, col = lax.axis_index("ctr"), lax.axis_index("row"), lax.axis_index("col")
    occ, virt = bounds_of(occ_ref), bounds_of(virt_ref)
    lanes = [irrep_lanes(at * FOLD, FOLD, virt) for at in range(4)]
    rows = irrep_rows(ctr * 128, 128, virt)
    irr_i = irrep(slab_ref[row], occ)
    for k in range(4):
        want = rows ^ (irr_i ^ irrep(k_ref[4 * col + k], occ))
        folded = fold_of(lambda at: t_ref[:, k, at * FOLD : (at + 1) * FOLD], want, lanes)
        out_ref[(ctr % 2) ^ (k // 2), k % 2] = folded.astype(out_ref.dtype)


def assemble(pieces, t_all):
    col, odd = lax.axis_index("col"), lax.axis_index("ctr") % 2
    for n, piece in enumerate(pieces):
        flip, u = (0, 2, 1, 3)[n // 2], n % 2
        for k in range(2):
            t_all[k, 2 * (col ^ flip) + (odd ^ u)] = piece[k]


def products(ahead, t_all, w, u, scalars):
    occ_ref, virt_ref, slab_ref, k_ref = scalars
    ctr, row = lax.axis_index("ctr"), lax.axis_index("row")
    occ, virt = bounds_of(occ_ref), bounds_of(virt_ref)
    irr_i = irrep(slab_ref[row], occ)
    away = [irr_i ^ irrep(k_ref[2 * ctr + k], occ) for k in range(2)]
    quarters = [row, (row + 3) % 4, (row + 1) % 4, (row + 2) % 4]
    at = [4 * h + (ctr + ahead) % 4 for h in range(2)]
    a_rows = [irrep_rows(block * 128, 128, virt) for block in at]
    a_lanes = [irrep_lanes(block * 128, 128, virt) for block in at]
    total = jnp.zeros((FOLD, 256), jnp.float32)
    for k in range(2):
        left = [t_all[k, block].astype(jnp.float32) for block in at]
        for n, q in enumerate(quarters):
            c_lanes = irrep_lanes(q * 256, 256, virt)
            right = jnp.concatenate(
                [jnp.where((a_rows[m] ^ away[k]) == c_lanes, left[m], 0.0) for m in range(2)], axis=0
            ).astype(t_all.dtype)
            total = total + lax.dot_general(
                w[n][k], right, (((1,), (1,)), ((), ())), preferred_element_type=jnp.float32
            )
            d_rows = irrep_rows(q * 256, 256, virt) ^ away[k]
            both = t_all[k, pl.ds(2 * q, 2)].reshape(256, FOLD).astype(jnp.float32)
            half = jnp.where(at[0] % 2 == 0, both[:, :128], both[:, 128:])
            right = jnp.concatenate(
                [jnp.where(d_rows == a_lanes[m], half, 0.0) for m in range(2)], axis=1
            ).astype(t_all.dtype)
            total = total + lax.dot_general(
                u[n][k], right, (((1,), (0,)), ((), ())), preferred_element_type=jnp.float32
            )
    return total


def split(refs):
    held = refs[1:6]
    w, u = [*(ref.at[0] for ref in held[:3]), held[3]], [*(ref.at[1] for ref in held[:3]), held[4]]
    return refs[0], w, u, refs[6:10], refs[10:]


def far_products(*refs):
    pieces, (_, w, u, scalars, (out, t_all)) = refs[:8], split(refs[7:])
    assemble(pieces, t_all)
    total = products(2, t_all, w, u, scalars)
    out[0], out[1] = total[:, :128], total[:, 128:]


def near_products(*refs):
    t_all, w, u, scalars, (out,) = split(refs)
    for n, ahead in enumerate((1, 3, 0)):
        total = products(ahead, t_all, w, u, scalars)
        out[n, 0], out[n, 1] = total[:, :128], total[:, 128:]


def finish(here, low, high, across_ref, occ_ref, virt_ref, slab_ref, j_ref, out_ref):
    ctr, row, col = lax.axis_index("ctr"), lax.axis_index("row"), lax.axis_index("col")
    occ, virt = bounds_of(occ_ref), bounds_of(virt_ref)
    h = ctr // 4
    total = (here[h] + low[h] + high[h] + across_ref[...]).T
    want = irrep_rows(ctr * 128, 128, virt) ^ (irrep(slab_ref[row], occ) ^ irrep(j_ref[col], occ))
    for at in range(4):
        kept = jnp.where(want == irrep_lanes(at * FOLD, FOLD, virt), total, 0.0)
        out_ref[:, at * FOLD : (at + 1) * FOLD] = kept.astype(out_ref.dtype)


def call(kernel, outs, arrays, scalars, scratch=(), place=VMEM, place_scalars=SMEM, mib=16, name=None):
    return pl.pallas_call(
        kernel,
        out_shape=[jax.ShapeDtypeStruct(*out) for out in outs],
        in_specs=[place] * len(arrays) + [place_scalars] * len(scalars),
        out_specs=[VMEM] * len(outs),
        scratch_shapes=scratch,
        compiler_params=pltpu.CompilerParams(vmem_limit_bytes=mib << 20),
        cost_estimate=pl.CostEstimate(flops=1 << 10, bytes_accessed=1 << 10, transcendentals=0),
        name=name,
    )(*arrays, *scalars)


def shift(value, axis, count, step):
    return lax.ppermute(value, axis, [(at, (at + step) % count) for at in range(count)])


def shift_y(value, step):
    return lax.ppermute(value, "ctr", [(at, at // 4 * 4 + (at + step) % 4) for at in range(8)])


def swap(value, axis, count, mask):
    return lax.ppermute(value, axis, [(at, at ^ mask) for at in range(count)])


def on_device(amps, w_cycle, w_cross, occ_sizes, virt_sizes, slab_occ, k_occ, j_occ):
    bf16, f32 = jnp.bfloat16, jnp.float32
    hbm = pl.BlockSpec(memory_space=pltpu.HBM)
    small = [occ_sizes, virt_sizes, k_occ, j_occ]
    own = call(
        fold_integrals, [((2, 2, FOLD, 256), bf16)], [w_cycle[:, :, 0], w_cross[:, :, 0]], small,
        [pltpu.VMEM((2, 256, 1024), bf16)] * 2
        + [pltpu.SMEM(value.shape, value.dtype) for value in small]
        + [pltpu.SemaphoreType.DMA((2, 2)), pltpu.SemaphoreType.DMA((4,))],
        place=hbm, place_scalars=hbm, mib=62, name="fold_integrals",
    )[0]
    up, down = shift(own, "row", 4, 1), shift(own, "row", 4, -1)
    integrals = [own, up, down, shift(up[0], "row", 4, 1), shift(down[1], "row", 4, -1)]

    t = call(
        fold_amplitudes, [((2, 2, 128, FOLD), bf16)], [amps[0]],
        [occ_sizes, virt_sizes, slab_occ, k_occ], name="fold_amplitudes",
    )[0]

    def spread(value, flip):
        pairs = [(x * 4 + q, (2 * q + (x % 2 ^ flip)) * 4 + x // 2) for x in range(8) for q in range(4)]
        return lax.ppermute(value, ("ctr", "col"), pairs)

    arrived = [spread(t[flip], flip) for flip in range(2)]
    beside = [swap(piece, "col", 4, 2) for piece in arrived]
    there = [swap(piece, "col", 4, 1) for piece in arrived]
    beyond = [swap(piece, "col", 4, 1) for piece in beside]
    pieces = [*arrived, *beside, *there, *beyond]
    scalars = [occ_sizes, virt_sizes, slab_occ, k_occ]

    far, t_all = call(
        far_products, [((2, FOLD, 128), f32), ((2, 8, 128, FOLD), bf16)], [*pieces, *integrals], scalars,
        name="far_products",
    )
    below, above = shift_y(far[0], 1), shift_y(far[1], -1)
    near = call(near_products, [((3, 2, FOLD, 128), f32)], [t_all, *integrals], scalars, name="near_products")[0]
    low = shift_y(near[0].at[0].add(below), 1)
    high = shift_y(near[1].at[1].add(above), -1)
    other = 1 - lax.axis_index("ctr") // 4
    pick = lambda value: lax.dynamic_index_in_dim(value, other, 0, False)
    across = swap(pick(near[2]) + pick(low) + pick(high), "ctr", 8, 4)
    out = call(
        finish, [((128, 4 * FOLD), bf16)], [near[2], low, high, across],
        [occ_sizes, virt_sizes, slab_occ, j_occ], name="finish",
    )[0]
    return out[None, :, None, :]


def solution(mesh):
    return jax.shard_map(
        on_device,
        mesh=mesh,
        in_specs=(
            P("row", "ctr", "col", None),
            P("ctr", "row", "col", None),
            P("ctr", "row", "col", None),
            P(),
            P(),
            P(),
            P(),
            P(),
        ),
        out_specs=P("row", "ctr", "col", None),
        check_vma=False,
    )
```

```python
import functools

import jax
import jax.numpy as jnp
from jax import lax
from jax.experimental import pallas as pl
from jax.experimental.pallas import tpu as pltpu
from jax.sharding import PartitionSpec as P

FOLD = 256
SMEM = pl.BlockSpec(memory_space=pltpu.SMEM)
VMEM = pl.BlockSpec(memory_space=pltpu.VMEM)


def bounds_of(sizes_ref):
    total, bounds = sizes_ref[0], []
    for g in range(1, 8):
        bounds.append(total)
        total = total + sizes_ref[g]
    return bounds


def bounds_in(table):
    return [table[g : g + 1, :1] for g in range(7)]


def irrep(index, bounds):
    total = (index >= bounds[0]).astype(jnp.int32)
    for bound in bounds[1:]:
        total = total + (index >= bound).astype(jnp.int32)
    return total


def irrep_lanes(start, count, bounds):
    return irrep(lax.broadcasted_iota(jnp.int32, (1, count), 1) + start, bounds)


def irrep_rows(start, count, bounds):
    return irrep(lax.broadcasted_iota(jnp.int32, (count, 1), 0) + start, bounds)


def fold_of(load, want, lanes):
    total = None
    for at, irr in enumerate(lanes):
        kept = jnp.where(want == irr, load(at).astype(jnp.float32), 0.0)
        total = kept if total is None else total + kept
    return total


def fold_integrals(w_hbm, u_hbm, *refs):
    small, (out_ref, table, w_ref, u_ref, *held, sems, small_sems) = refs[:5], refs[5:]
    fetch = [pltpu.make_async_copy(*pair, small_sems.at[n]) for n, pair in enumerate(zip(small, held))]
    copies = [
        [
            pltpu.make_async_copy(hbm.at[k], ref.at[k], sems.at[k, n])
            for n, (hbm, ref) in enumerate(((w_hbm, w_ref), (u_hbm, u_ref)))
        ]
        for k in range(2)
    ]
    for copy in [*fetch, *copies[0], *copies[1]]:
        copy.start()
    for copy in fetch:
        copy.wait()
    occ_ref, virt_ref, slab_ref, k_ref, j_ref = held
    ctr, row, col = lax.axis_index("ctr"), lax.axis_index("row"), lax.axis_index("col")
    occ, virt = bounds_of(occ_ref), bounds_of(virt_ref)
    irr_i = irrep(slab_ref[row], occ)
    entries = [*virt, *(irr_i ^ irrep(k_ref[2 * ctr + k], occ) for k in range(2)), irr_i ^ irrep(j_ref[col], occ)]
    line = lax.broadcasted_iota(jnp.int32, table.shape, 0)
    held_table = jnp.zeros(table.shape, jnp.int32)
    for n, entry in enumerate(entries):
        held_table = jnp.where(line == n, entry, held_table)
    table[...] = held_table
    lanes = [irrep_lanes(at * FOLD, FOLD, virt) for at in range(4)]
    rows = irrep_rows(row * 256, 256, virt)
    irr_j = irrep(j_ref[col], occ)
    for k in range(2):
        want = rows ^ (irr_j ^ irrep(k_ref[2 * ctr + k], occ))
        for n, ref in enumerate((w_ref, u_ref)):
            copies[k][n].wait()
            folded = fold_of(lambda at: ref[k, :, at * FOLD : (at + 1) * FOLD], want, lanes)
            out_ref[n, k] = folded.T.astype(out_ref.dtype)


def fold_amplitudes(t_ref, occ_ref, virt_ref, slab_ref, k_ref, out_ref):
    ctr, row, col = lax.axis_index("ctr"), lax.axis_index("row"), lax.axis_index("col")
    occ, virt = bounds_of(occ_ref), bounds_of(virt_ref)
    lanes = [irrep_lanes(at * FOLD, FOLD, virt) for at in range(4)]
    rows = irrep_rows(ctr * 128, 128, virt)
    irr_i = irrep(slab_ref[row], occ)
    for k in range(4):
        want = rows ^ (irr_i ^ irrep(k_ref[4 * col + k], occ))
        folded = fold_of(lambda at: t_ref[:, k, at * FOLD : (at + 1) * FOLD], want, lanes)
        out_ref[(ctr % 2) ^ (k // 2), k % 2] = folded.astype(out_ref.dtype)


def assemble(pieces, t_all):
    col, odd = lax.axis_index("col"), lax.axis_index("ctr") % 2
    for n, piece in enumerate(pieces):
        flip, u = (0, 2, 1, 3)[n // 2], n % 2
        for k in range(2):
            t_all[k, 2 * (col ^ flip) + (odd ^ u)] = piece[k]


def products(ahead, t_all, w, u, table):
    ctr, row = lax.axis_index("ctr"), lax.axis_index("row")
    virt = bounds_in(table)
    quarters = [row, (row + 3) % 4, (row + 1) % 4, (row + 2) % 4]
    at = [4 * h + (ctr + ahead) % 4 for h in range(2)]
    dtype = t_all.dtype
    small = lambda value: value.astype(jnp.float32).astype(dtype)
    a_lanes = [small(irrep_lanes(block * 128, 128, virt)) for block in at]
    q_lanes = [small(irrep_lanes(q * 256, 256, virt)) for q in quarters]
    zero = jnp.zeros((), dtype)
    total = None
    for k in range(2):
        away = table[7 + k : 8 + k, :1]
        a_rows = jnp.concatenate([small(irrep_rows(block * 128, 128, virt) ^ away) for block in at], axis=0)
        left = jnp.concatenate([t_all[k, block] for block in at], axis=0)
        right = jnp.concatenate([jnp.where(a_rows == lanes, left, zero) for lanes in q_lanes], axis=1)
        part = lax.dot_general(
            jnp.concatenate([w[n][k] for n in range(4)], axis=1), right, (((1,), (1,)), ((), ())),
            preferred_element_type=jnp.float32,
        )
        total = part if total is None else total + part
        right = []
        for q in quarters:
            d_rows = small(irrep_rows(q * 256, 256, virt) ^ away)
            half = t_all[k, pl.ds(2 * q, 2)].reshape(256, FOLD)
            half = jnp.where(at[0] % 2 == 0, half[:, :128], half[:, 128:])
            right.append(jnp.concatenate([jnp.where(d_rows == lanes, half, zero) for lanes in a_lanes], axis=1))
        total = total + lax.dot_general(
            jnp.concatenate([u[n][k] for n in range(4)], axis=1), jnp.concatenate(right, axis=0),
            (((1,), (0,)), ((), ())), preferred_element_type=jnp.float32,
        )
    return total


def split(refs):
    held = refs[1:6]
    w, u = [*(ref.at[0] for ref in held[:3]), held[3]], [*(ref.at[1] for ref in held[:3]), held[4]]
    return refs[0], w, u, refs[6], refs[7:]


def far_products(*refs):
    pieces, (_, w, u, table, (out, t_all)) = refs[:8], split(refs[7:])
    assemble(pieces, t_all)
    total = products(2, t_all, w, u, table)
    out[0], out[1] = total[:, :128], total[:, 128:]


def near_products(*refs):
    t_all, w, u, table, (out,) = split(refs)
    for n, ahead in enumerate((1, 3, 0)):
        total = products(ahead, t_all, w, u, table)
        out[n, 0], out[n, 1] = total[:, :128], total[:, 128:]


def finish(here, low, high, across_ref, table, out_ref):
    virt, ctr = bounds_in(table), lax.axis_index("ctr")
    h = ctr // 4
    total = (here[h] + low[h] + high[h] + across_ref[...]).T
    want = irrep_rows(ctr * 128, 128, virt) ^ table[9:10, :1]
    for at in range(4):
        kept = jnp.where(want == irrep_lanes(at * FOLD, FOLD, virt), total, 0.0)
        out_ref[:, at * FOLD : (at + 1) * FOLD] = kept.astype(out_ref.dtype)


def call(kernel, outs, arrays, scalars, scratch=(), place=VMEM, place_scalars=SMEM, mib=16, flops=1 << 10, name=None):
    return pl.pallas_call(
        kernel,
        out_shape=[jax.ShapeDtypeStruct(*out) for out in outs],
        in_specs=[place] * len(arrays) + [place_scalars] * len(scalars),
        out_specs=[VMEM] * len(outs),
        scratch_shapes=scratch,
        compiler_params=pltpu.CompilerParams(vmem_limit_bytes=mib << 20),
        cost_estimate=pl.CostEstimate(flops=flops, bytes_accessed=1 << 10, transcendentals=0),
        name=name,
    )(*arrays, *scalars)


def shift(value, axis, count, step):
    return lax.ppermute(value, axis, [(at, (at + step) % count) for at in range(count)])


def shift_y(value, step):
    return lax.ppermute(value, "ctr", [(at, at // 4 * 4 + (at + step) % 4) for at in range(8)])


def swap(value, axis, count, mask):
    return lax.ppermute(value, axis, [(at, at ^ mask) for at in range(count)])


def on_device(amps, w_cycle, w_cross, occ_sizes, virt_sizes, slab_occ, k_occ, j_occ):
    bf16, f32 = jnp.bfloat16, jnp.float32
    hbm = pl.BlockSpec(memory_space=pltpu.HBM)
    small = [occ_sizes, virt_sizes, slab_occ, k_occ, j_occ]
    own, table = call(
        fold_integrals, [((2, 2, FOLD, 256), bf16), ((16, 128), jnp.int32)], [w_cycle[:, :, 0], w_cross[:, :, 0]], small,
        [pltpu.VMEM((2, 256, 1024), bf16)] * 2
        + [pltpu.SMEM(value.shape, value.dtype) for value in small]
        + [pltpu.SemaphoreType.DMA((2, 2)), pltpu.SemaphoreType.DMA((5,))],
        place=hbm, place_scalars=hbm, mib=62, name="fold_integrals",
    )
    up, down = shift(own, "row", 4, 1), shift(own, "row", 4, -1)
    w_far, u_far = shift(up[0], "row", 4, 1), shift(down[1], "row", 4, -1)
    integrals = [own, up, down, w_far, u_far]

    t = call(
        fold_amplitudes, [((2, 2, 128, FOLD), bf16)], [amps[0]],
        [occ_sizes, virt_sizes, slab_occ, k_occ], name="fold_amplitudes",
    )[0]

    def spread(value, flip):
        pairs = [(x * 4 + q, (2 * q + (x % 2 ^ flip)) * 4 + x // 2) for x in range(8) for q in range(4)]
        return lax.ppermute(value, ("ctr", "col"), pairs)

    arrived = [spread(t[flip], flip) for flip in range(2)]
    beside = [swap(piece, "col", 4, 2) for piece in arrived]
    there = [swap(piece, "col", 4, 1) for piece in arrived]
    beyond = [swap(piece, "col", 4, 1) for piece in beside]
    pieces = [*arrived, *beside, *there, *beyond]

    far, t_all = call(
        far_products, [((2, FOLD, 128), f32), ((2, 8, 128, FOLD), bf16)], [*pieces, *integrals, table], [],
        name="far_products",
    )
    below, above = shift_y(far[0], 1), shift_y(far[1], -1)
    near = call(near_products, [((3, 2, FOLD, 128), f32)], [t_all, *integrals, table], [], name="near_products")[0]
    low = shift_y(near[0].at[0].add(below), 1)
    high = shift_y(near[1].at[1].add(above), -1)
    other = 1 - lax.axis_index("ctr") // 4
    pick = lambda value: lax.dynamic_index_in_dim(value, other, 0, False)
    across = swap(pick(near[2]) + pick(low) + pick(high), "ctr", 8, 4)
    out = call(finish, [((128, 4 * FOLD), bf16)], [near[2], low, high, across, table], [], name="finish")[0]
    return out[None, :, None, :]


def solution(mesh):
    return jax.shard_map(
        on_device,
        mesh=mesh,
        in_specs=(
            P("row", "ctr", "col", None),
            P("ctr", "row", "col", None),
            P("ctr", "row", "col", None),
            P(),
            P(),
            P(),
            P(),
            P(),
        ),
        out_specs=P("row", "ctr", "col", None),
        check_vma=False,
    )
```

```python
import functools

import jax
import jax.numpy as jnp
from jax import lax
from jax.experimental import pallas as pl
from jax.experimental.pallas import tpu as pltpu
from jax.sharding import PartitionSpec as P

FOLD = 256
SMEM = pl.BlockSpec(memory_space=pltpu.SMEM)
VMEM = pl.BlockSpec(memory_space=pltpu.VMEM)


def bounds_of(sizes_ref):
    total, bounds = sizes_ref[0], []
    for g in range(1, 8):
        bounds.append(total)
        total = total + sizes_ref[g]
    return bounds


def bounds_in(table):
    return [table[g : g + 1, :1] for g in range(7)]


def irrep(index, bounds):
    total = (index >= bounds[0]).astype(jnp.int32)
    for bound in bounds[1:]:
        total = total + (index >= bound).astype(jnp.int32)
    return total


def irrep_lanes(start, count, bounds):
    return irrep(lax.broadcasted_iota(jnp.int32, (1, count), 1) + start, bounds)


def irrep_rows(start, count, bounds):
    return irrep(lax.broadcasted_iota(jnp.int32, (count, 1), 0) + start, bounds)


def fold_of(load, want, lanes):
    total = None
    for at, irr in enumerate(lanes):
        kept = jnp.where(want == irr, load(at).astype(jnp.float32), 0.0)
        total = kept if total is None else total + kept
    return total


def fold_integrals(w_hbm, u_hbm, *refs):
    small, (out_ref, table, w_ref, u_ref, *held, sems, small_sems) = refs[:5], refs[5:]
    fetch = [pltpu.make_async_copy(*pair, small_sems.at[n]) for n, pair in enumerate(zip(small, held))]
    copies = [
        [
            pltpu.make_async_copy(hbm.at[k], ref.at[k], sems.at[k, n])
            for n, (hbm, ref) in enumerate(((w_hbm, w_ref), (u_hbm, u_ref)))
        ]
        for k in range(2)
    ]
    for copy in [*fetch, *copies[0], *copies[1]]:
        copy.start()
    for copy in fetch:
        copy.wait()
    occ_ref, virt_ref, slab_ref, k_ref, j_ref = held
    ctr, row, col = lax.axis_index("ctr"), lax.axis_index("row"), lax.axis_index("col")
    occ, virt = bounds_of(occ_ref), bounds_of(virt_ref)
    irr_i = irrep(slab_ref[row], occ)
    entries = [*virt, *(irr_i ^ irrep(k_ref[2 * ctr + k], occ) for k in range(2)), irr_i ^ irrep(j_ref[col], occ)]
    line = lax.broadcasted_iota(jnp.int32, table.shape, 0)
    held_table = jnp.zeros(table.shape, jnp.int32)
    for n, entry in enumerate(entries):
        held_table = jnp.where(line == n, entry, held_table)
    table[...] = held_table
    dtype = w_ref.dtype
    small = lambda value: value.astype(jnp.float32).astype(dtype)
    lanes = [small(irrep_lanes(at * FOLD, FOLD, virt)) for at in range(4)]
    rows = irrep_rows(row * 256, 256, virt)
    irr_j = irrep(j_ref[col], occ)
    for k in range(2):
        want = small(rows ^ (irr_j ^ irrep(k_ref[2 * ctr + k], occ)))
        for n, ref in enumerate((w_ref, u_ref)):
            copies[k][n].wait()
            total = None
            for at, irr in enumerate(lanes):
                kept = jnp.where(want == irr, ref[k, :, at * FOLD : (at + 1) * FOLD], jnp.zeros((), dtype))
                total = kept if total is None else total + kept
            out_ref[n, k] = total.T


def fold_amplitudes(t_ref, occ_ref, virt_ref, slab_ref, k_ref, out_ref):
    ctr, row, col = lax.axis_index("ctr"), lax.axis_index("row"), lax.axis_index("col")
    occ, virt = bounds_of(occ_ref), bounds_of(virt_ref)
    lanes = [irrep_lanes(at * FOLD, FOLD, virt) for at in range(4)]
    rows = irrep_rows(ctr * 128, 128, virt)
    irr_i = irrep(slab_ref[row], occ)
    for k in range(4):
        want = rows ^ (irr_i ^ irrep(k_ref[4 * col + k], occ))
        folded = fold_of(lambda at: t_ref[:, k, at * FOLD : (at + 1) * FOLD], want, lanes)
        out_ref[(ctr % 2) ^ (k // 2), k % 2] = folded.astype(out_ref.dtype)


def assemble(pieces, t_all):
    col, odd = lax.axis_index("col"), lax.axis_index("ctr") % 2
    for n, piece in enumerate(pieces):
        flip, u = (0, 2, 1, 3)[n // 2], n % 2
        for k in range(2):
            t_all[k, 2 * (col ^ flip) + (odd ^ u)] = piece[k]


def products(ahead, t_all, w, u, table):
    ctr, row = lax.axis_index("ctr"), lax.axis_index("row")
    virt = bounds_in(table)
    quarters = [row, (row + 3) % 4, (row + 1) % 4, (row + 2) % 4]
    at = [4 * h + (ctr + ahead) % 4 for h in range(2)]
    dtype = t_all.dtype
    small = lambda value: value.astype(jnp.float32).astype(dtype)
    a_lanes = [small(irrep_lanes(block * 128, 128, virt)) for block in at]
    q_lanes = [small(irrep_lanes(q * 256, 256, virt)) for q in quarters]
    zero = jnp.zeros((), dtype)
    total = None
    for k in range(2):
        away = table[7 + k : 8 + k, :1]
        a_rows = jnp.concatenate([small(irrep_rows(block * 128, 128, virt) ^ away) for block in at], axis=0)
        left = jnp.concatenate([t_all[k, block] for block in at], axis=0)
        right = jnp.concatenate([jnp.where(a_rows == lanes, left, zero) for lanes in q_lanes], axis=1)
        part = lax.dot_general(
            jnp.concatenate([w[n][k] for n in range(4)], axis=1), right, (((1,), (1,)), ((), ())),
            preferred_element_type=jnp.float32,
        )
        total = part if total is None else total + part
        right = []
        for q in quarters:
            d_rows = small(irrep_rows(q * 256, 256, virt) ^ away)
            half = t_all[k, pl.ds(2 * q, 2)].reshape(256, FOLD)
            half = jnp.where(at[0] % 2 == 0, half[:, :128], half[:, 128:])
            right.append(jnp.concatenate([jnp.where(d_rows == lanes, half, zero) for lanes in a_lanes], axis=1))
        total = total + lax.dot_general(
            jnp.concatenate([u[n][k] for n in range(4)], axis=1), jnp.concatenate(right, axis=0),
            (((1,), (0,)), ((), ())), preferred_element_type=jnp.float32,
        )
    return total


def split(refs):
    held = refs[1:6]
    w, u = [*(ref.at[0] for ref in held[:3]), held[3]], [*(ref.at[1] for ref in held[:3]), held[4]]
    return refs[0], w, u, refs[6], refs[7:]


def far_products(*refs):
    pieces, (_, w, u, table, (out, t_all)) = refs[:8], split(refs[7:])
    assemble(pieces, t_all)
    total = products(2, t_all, w, u, table)
    out[0], out[1] = total[:, :128], total[:, 128:]


def near_products(*refs):
    t_all, w, u, table, (out,) = split(refs)
    for n, ahead in enumerate((1, 3, 0)):
        total = products(ahead, t_all, w, u, table)
        out[n, 0], out[n, 1] = total[:, :128], total[:, 128:]


def finish(here, low, high, across_ref, table, out_ref):
    virt, ctr = bounds_in(table), lax.axis_index("ctr")
    h = ctr // 4
    total = (here[h] + low[h] + high[h] + across_ref[...]).T
    want = irrep_rows(ctr * 128, 128, virt) ^ table[9:10, :1]
    for at in range(4):
        kept = jnp.where(want == irrep_lanes(at * FOLD, FOLD, virt), total, 0.0)
        out_ref[:, at * FOLD : (at + 1) * FOLD] = kept.astype(out_ref.dtype)


def call(kernel, outs, arrays, scalars, scratch=(), place=VMEM, place_scalars=SMEM, mib=16, flops=1 << 10, name=None):
    return pl.pallas_call(
        kernel,
        out_shape=[jax.ShapeDtypeStruct(*out) for out in outs],
        in_specs=[place] * len(arrays) + [place_scalars] * len(scalars),
        out_specs=[VMEM] * len(outs),
        scratch_shapes=scratch,
        compiler_params=pltpu.CompilerParams(vmem_limit_bytes=mib << 20),
        cost_estimate=pl.CostEstimate(flops=flops, bytes_accessed=1 << 10, transcendentals=0),
        name=name,
    )(*arrays, *scalars)


def shift(value, axis, count, step):
    return lax.ppermute(value, axis, [(at, (at + step) % count) for at in range(count)])


def shift_y(value, step):
    return lax.ppermute(value, "ctr", [(at, at // 4 * 4 + (at + step) % 4) for at in range(8)])


def swap(value, axis, count, mask):
    return lax.ppermute(value, axis, [(at, at ^ mask) for at in range(count)])


def on_device(amps, w_cycle, w_cross, occ_sizes, virt_sizes, slab_occ, k_occ, j_occ):
    bf16, f32 = jnp.bfloat16, jnp.float32
    hbm = pl.BlockSpec(memory_space=pltpu.HBM)
    small = [occ_sizes, virt_sizes, slab_occ, k_occ, j_occ]
    own, table = call(
        fold_integrals, [((2, 2, FOLD, 256), bf16), ((16, 128), jnp.int32)], [w_cycle[:, :, 0], w_cross[:, :, 0]], small,
        [pltpu.VMEM((2, 256, 1024), bf16)] * 2
        + [pltpu.SMEM(value.shape, value.dtype) for value in small]
        + [pltpu.SemaphoreType.DMA((2, 2)), pltpu.SemaphoreType.DMA((5,))],
        place=hbm, place_scalars=hbm, mib=62, name="fold_integrals",
    )
    up, down = shift(own, "row", 4, 1), shift(own, "row", 4, -1)
    w_far, u_far = shift(up[0], "row", 4, 1), shift(down[1], "row", 4, -1)
    integrals = [own, up, down, w_far, u_far]

    t = call(
        fold_amplitudes, [((2, 2, 128, FOLD), bf16)], [amps[0]],
        [occ_sizes, virt_sizes, slab_occ, k_occ], name="fold_amplitudes",
    )[0]

    def spread(value, flip):
        pairs = [(x * 4 + q, (2 * q + (x % 2 ^ flip)) * 4 + x // 2) for x in range(8) for q in range(4)]
        return lax.ppermute(value, ("ctr", "col"), pairs)

    arrived = [spread(t[flip], flip) for flip in range(2)]
    beside = [swap(piece, "col", 4, 2) for piece in arrived]
    there = [swap(piece, "col", 4, 1) for piece in arrived]
    beyond = [swap(piece, "col", 4, 1) for piece in beside]
    pieces = [*arrived, *beside, *there, *beyond]

    far, t_all = call(
        far_products, [((2, FOLD, 128), f32), ((2, 8, 128, FOLD), bf16)], [*pieces, *integrals, table], [],
        name="far_products",
    )
    below, above = shift_y(far[0], 1), shift_y(far[1], -1)
    near = call(near_products, [((3, 2, FOLD, 128), f32)], [t_all, *integrals, table], [], name="near_products")[0]
    low = shift_y(near[0].at[0].add(below), 1)
    high = shift_y(near[1].at[1].add(above), -1)
    other = 1 - lax.axis_index("ctr") // 4
    pick = lambda value: lax.dynamic_index_in_dim(value, other, 0, False)
    across = swap(pick(near[2]) + pick(low) + pick(high), "ctr", 8, 4)
    out = call(finish, [((128, 4 * FOLD), bf16)], [near[2], low, high, across, table], [], name="finish")[0]
    return out[None, :, None, :]


def solution(mesh):
    return jax.shard_map(
        on_device,
        mesh=mesh,
        in_specs=(
            P("row", "ctr", "col", None),
            P("ctr", "row", "col", None),
            P("ctr", "row", "col", None),
            P(),
            P(),
            P(),
            P(),
            P(),
        ),
        out_specs=P("row", "ctr", "col", None),
        check_vma=False,
    )
```

```python
import functools

import jax
import jax.numpy as jnp
from jax import lax
from jax.experimental import pallas as pl
from jax.experimental.pallas import tpu as pltpu
from jax.sharding import PartitionSpec as P

FOLD = 256
SMEM = pl.BlockSpec(memory_space=pltpu.SMEM)
VMEM = pl.BlockSpec(memory_space=pltpu.VMEM)


def bounds_of(sizes_ref):
    total, bounds = sizes_ref[0], []
    for g in range(1, 8):
        bounds.append(total)
        total = total + sizes_ref[g]
    return bounds


def bounds_in(table):
    return [table[g : g + 1, :1] for g in range(7)]


def irrep(index, bounds):
    total = (index >= bounds[0]).astype(jnp.int32)
    for bound in bounds[1:]:
        total = total + (index >= bound).astype(jnp.int32)
    return total


def irrep_lanes(start, count, bounds):
    return irrep(lax.broadcasted_iota(jnp.int32, (1, count), 1) + start, bounds)


def irrep_rows(start, count, bounds):
    return irrep(lax.broadcasted_iota(jnp.int32, (count, 1), 0) + start, bounds)


def fold_of(load, want, lanes):
    total = None
    for at, irr in enumerate(lanes):
        kept = jnp.where(want == irr, load(at).astype(jnp.float32), 0.0)
        total = kept if total is None else total + kept
    return total


def fold_integrals(w_hbm, u_hbm, *refs):
    small, (out_ref, table, w_ref, u_ref, *held, sems, small_sems) = refs[:5], refs[5:]
    fetch = [pltpu.make_async_copy(*pair, small_sems.at[n]) for n, pair in enumerate(zip(small, held))]
    copies = [
        [
            pltpu.make_async_copy(hbm.at[k], ref.at[k], sems.at[k, n])
            for n, (hbm, ref) in enumerate(((w_hbm, w_ref), (u_hbm, u_ref)))
        ]
        for k in range(2)
    ]
    for copy in [*fetch, *copies[0], *copies[1]]:
        copy.start()
    for copy in fetch:
        copy.wait()
    occ_ref, virt_ref, slab_ref, k_ref, j_ref = held
    ctr, row, col = lax.axis_index("ctr"), lax.axis_index("row"), lax.axis_index("col")
    occ, virt = bounds_of(occ_ref), bounds_of(virt_ref)
    irr_i = irrep(slab_ref[row], occ)
    entries = [*virt, *(irr_i ^ irrep(k_ref[2 * ctr + k], occ) for k in range(2)), irr_i ^ irrep(j_ref[col], occ)]
    line = lax.broadcasted_iota(jnp.int32, table.shape, 0)
    held_table = jnp.zeros(table.shape, jnp.int32)
    for n, entry in enumerate(entries):
        held_table = jnp.where(line == n, entry, held_table)
    table[...] = held_table
    dtype = w_ref.dtype
    small = lambda value: value.astype(jnp.float32).astype(dtype)
    lanes = [small(irrep_lanes(at * FOLD, FOLD, virt)) for at in range(4)]
    rows = irrep_rows(row * 256, 256, virt)
    irr_j = irrep(j_ref[col], occ)
    for k in range(2):
        want = small(rows ^ (irr_j ^ irrep(k_ref[2 * ctr + k], occ)))
        for n, ref in enumerate((w_ref, u_ref)):
            copies[k][n].wait()
            total = None
            for at, irr in enumerate(lanes):
                kept = jnp.where(want == irr, ref[k, :, at * FOLD : (at + 1) * FOLD], jnp.zeros((), dtype))
                total = kept if total is None else total + kept
            out_ref[n, k] = total.T


def fold_amplitudes(t_ref, occ_ref, virt_ref, slab_ref, k_ref, out_ref):
    ctr, row, col = lax.axis_index("ctr"), lax.axis_index("row"), lax.axis_index("col")
    occ, virt = bounds_of(occ_ref), bounds_of(virt_ref)
    lanes = [irrep_lanes(at * FOLD, FOLD, virt) for at in range(4)]
    rows = irrep_rows(ctr * 128, 128, virt)
    irr_i = irrep(slab_ref[row], occ)
    for k in range(4):
        want = rows ^ (irr_i ^ irrep(k_ref[4 * col + k], occ))
        folded = fold_of(lambda at: t_ref[:, k, at * FOLD : (at + 1) * FOLD], want, lanes)
        out_ref[(ctr % 2) ^ (k // 2), k % 2] = folded.astype(out_ref.dtype)


def assemble(pieces, t_all):
    col, odd = lax.axis_index("col"), lax.axis_index("ctr") % 2
    for n, piece in enumerate(pieces):
        flip, u = (0, 2, 1, 3)[n // 2], n % 2
        for k in range(2):
            t_all[k, 2 * (col ^ flip) + (odd ^ u)] = piece[k]


def products(ahead, t_all, w, u, table):
    ctr, row = lax.axis_index("ctr"), lax.axis_index("row")
    virt = bounds_in(table)
    quarters = [row, (row + 3) % 4, (row + 1) % 4, (row + 2) % 4]
    at = [4 * h + (ctr + ahead) % 4 for h in range(2)]
    dtype = t_all.dtype
    small = lambda value: value.astype(jnp.float32).astype(dtype)
    a_lanes = [small(irrep_lanes(block * 128, 128, virt)) for block in at]
    q_lanes = [small(irrep_lanes(q * 256, 256, virt)) for q in quarters]
    zero = jnp.zeros((), dtype)
    total = None
    for k in range(2):
        away = table[7 + k : 8 + k, :1]
        a_rows = jnp.concatenate([small(irrep_rows(block * 128, 128, virt) ^ away) for block in at], axis=0)
        left = jnp.concatenate([t_all[k, block] for block in at], axis=0)
        right = jnp.concatenate([jnp.where(a_rows == lanes, left, zero) for lanes in q_lanes], axis=1)
        part = lax.dot_general(
            jnp.concatenate([w[n][k] for n in range(4)], axis=1), right, (((1,), (1,)), ((), ())),
            preferred_element_type=jnp.float32,
        )
        total = part if total is None else total + part
        right = []
        for q in quarters:
            d_rows = small(irrep_rows(q * 256, 256, virt) ^ away)
            half = t_all[k, pl.ds(2 * q, 2)].reshape(256, FOLD)
            half = jnp.where(at[0] % 2 == 0, half[:, :128], half[:, 128:])
            right.append(jnp.concatenate([jnp.where(d_rows == lanes, half, zero) for lanes in a_lanes], axis=1))
        total = total + lax.dot_general(
            jnp.concatenate([u[n][k] for n in range(4)], axis=1), jnp.concatenate(right, axis=0),
            (((1,), (0,)), ((), ())), preferred_element_type=jnp.float32,
        )
    return total


def split(refs):
    held = refs[1:6]
    w, u = [*(ref.at[0] for ref in held[:3]), held[3]], [*(ref.at[1] for ref in held[:3]), held[4]]
    return refs[0], w, u, refs[6], refs[7:]


def far_products(*refs):
    pieces, (_, w, u, table, (out, t_all)) = refs[:8], split(refs[7:])
    assemble(pieces, t_all)
    total = products(2, t_all, w, u, table)
    out[0], out[1] = total[:, :128], total[:, 128:]


def near_products(*refs):
    t_all, w, u, table, (out,) = split(refs)
    for n, ahead in enumerate((1, 3, 0)):
        total = products(ahead, t_all, w, u, table)
        out[n, 0], out[n, 1] = total[:, :128], total[:, 128:]


def finish(here, low, high, across_ref, table, out_ref):
    virt, ctr = bounds_in(table), lax.axis_index("ctr")
    h = ctr // 4
    total = (here[h] + low[...] + high[...] + across_ref[...]).T
    want = irrep_rows(ctr * 128, 128, virt) ^ table[9:10, :1]
    for at in range(4):
        kept = jnp.where(want == irrep_lanes(at * FOLD, FOLD, virt), total, 0.0)
        out_ref[:, at * FOLD : (at + 1) * FOLD] = kept.astype(out_ref.dtype)


def call(kernel, outs, arrays, scalars, scratch=(), place=VMEM, place_scalars=SMEM, mib=16, flops=1 << 10, name=None):
    return pl.pallas_call(
        kernel,
        out_shape=[jax.ShapeDtypeStruct(*out) for out in outs],
        in_specs=[place] * len(arrays) + [place_scalars] * len(scalars),
        out_specs=[VMEM] * len(outs),
        scratch_shapes=scratch,
        compiler_params=pltpu.CompilerParams(vmem_limit_bytes=mib << 20),
        cost_estimate=pl.CostEstimate(flops=flops, bytes_accessed=1 << 10, transcendentals=0),
        name=name,
    )(*arrays, *scalars)


def shift(value, axis, count, step):
    return lax.ppermute(value, axis, [(at, (at + step) % count) for at in range(count)])


def shift_y(value, step):
    return lax.ppermute(value, "ctr", [(at, at // 4 * 4 + (at + step) % 4) for at in range(8)])


def swap(value, axis, count, mask):
    return lax.ppermute(value, axis, [(at, at ^ mask) for at in range(count)])


def on_device(amps, w_cycle, w_cross, occ_sizes, virt_sizes, slab_occ, k_occ, j_occ):
    bf16, f32 = jnp.bfloat16, jnp.float32
    hbm = pl.BlockSpec(memory_space=pltpu.HBM)
    small = [occ_sizes, virt_sizes, slab_occ, k_occ, j_occ]
    own, table = call(
        fold_integrals, [((2, 2, FOLD, 256), bf16), ((16, 128), jnp.int32)], [w_cycle[:, :, 0], w_cross[:, :, 0]], small,
        [pltpu.VMEM((2, 256, 1024), bf16)] * 2
        + [pltpu.SMEM(value.shape, value.dtype) for value in small]
        + [pltpu.SemaphoreType.DMA((2, 2)), pltpu.SemaphoreType.DMA((5,))],
        place=hbm, place_scalars=hbm, mib=62, name="fold_integrals",
    )
    up, down = shift(own, "row", 4, 1), shift(own, "row", 4, -1)
    w_far, u_far = shift(up[0], "row", 4, 1), shift(down[1], "row", 4, -1)
    integrals = [own, up, down, w_far, u_far]

    t = call(
        fold_amplitudes, [((2, 2, 128, FOLD), bf16)], [amps[0]],
        [occ_sizes, virt_sizes, slab_occ, k_occ], name="fold_amplitudes",
    )[0]

    def spread(value, flip):
        pairs = [(x * 4 + q, (2 * q + (x % 2 ^ flip)) * 4 + x // 2) for x in range(8) for q in range(4)]
        return lax.ppermute(value, ("ctr", "col"), pairs)

    arrived = [spread(t[flip], flip) for flip in range(2)]
    beside = [swap(piece, "col", 4, 2) for piece in arrived]
    there = [swap(piece, "col", 4, 1) for piece in arrived]
    beyond = [swap(piece, "col", 4, 1) for piece in beside]
    pieces = [*arrived, *beside, *there, *beyond]

    far, t_all = call(
        far_products, [((2, FOLD, 128), f32), ((2, 8, 128, FOLD), bf16)], [*pieces, *integrals, table], [],
        name="far_products",
    )
    below, above = shift_y(far[0], 1), shift_y(far[1], -1)
    near = call(near_products, [((3, 2, FOLD, 128), f32)], [t_all, *integrals, table], [], name="near_products")[0]
    low1, high0 = shift_y(near[0, 1], 1), shift_y(near[1, 0], -1)
    low0, high1 = shift_y(near[0, 0] + below, 1), shift_y(near[1, 1] + above, -1)
    first = lax.axis_index("ctr") // 4 == 0
    mine = [jnp.where(first, low0, low1), jnp.where(first, high0, high1)]
    across = near[2, 0] + low0 + high0, near[2, 1] + low1 + high1
    across = swap(jnp.where(first, across[1], across[0]), "ctr", 8, 4)
    out = call(finish, [((128, 4 * FOLD), bf16)], [near[2], *mine, across, table], [], name="finish")[0]
    return out[None, :, None, :]


def solution(mesh):
    return jax.shard_map(
        on_device,
        mesh=mesh,
        in_specs=(
            P("row", "ctr", "col", None),
            P("ctr", "row", "col", None),
            P("ctr", "row", "col", None),
            P(),
            P(),
            P(),
            P(),
            P(),
        ),
        out_specs=P("row", "ctr", "col", None),
        check_vma=False,
    )
```
